256 devices in a mesh: row: 8 (over z), col: 32 (over y, x, core).
Axes of the slice: x: 4, y: 4, z: 8, core: 2. Of those that a mesh axis runs over, the one named last changes fastest.
Arguments:
- matrix: bfloat16 [6, 4096, 2, 16384], P(None, 'row', None, 'col'), may hold values from -6 to 6
- lower_inv: bfloat16 [2, 512, 512], replicated, as said below
- upper_inv: bfloat16 [2, 512, 512], replicated, as said below
Outputs:
- factored: bfloat16 [6, 4096, 2, 16384], P(None, 'row', None, 'col')
The draws below stay inside these ranges and needn't reach their ends.
Inputs may be any that keep to these rules, and one draw needn't show every extreme that they name: Each lower_inv[k] is unit lower triangular. Each upper_inv[k] is upper triangular with a positive diagonal.
All inputs are finite; a program needn't handle non-finite values.
Results may differ from the reference program's by a relative error of at most 0.0076.
Values may be sent and summed in bfloat16 or wider, within the bound.
A program may use at most 128 MiB of HBM per device.

```python
import math
import jax
import jax.numpy as jnp
from jax import lax

NB = 512
TR = 6
TC = 2
ROWS = 24576
COLS = 32768
N_ROW = 8
N_COL = 32


def draw_lower_inv(key, part):
    key = jax.random.fold_in(key, 11)
    offdiag = jax.random.normal(key, (2, NB, NB), jnp.float32) * (0.6 / math.sqrt(NB))
    row_pos = lax.broadcasted_iota(jnp.int32, (2, NB, NB), 1)
    col_pos = lax.broadcasted_iota(jnp.int32, (2, NB, NB), 2)
    values = jnp.where(row_pos > col_pos, offdiag, jnp.where(row_pos == col_pos, 1.0, 0.0))
    return values.astype(jnp.bfloat16)


def draw_upper_inv(key, part):
    key = jax.random.fold_in(key, 23)
    key_off, key_diag = jax.random.split(key)
    offdiag = jax.random.normal(key_off, (2, NB, NB), jnp.float32) * (0.5 / NB)
    diagonal = jnp.exp(jax.random.uniform(key_diag, (2, NB, 1), jnp.float32, math.log(0.5), math.log(2.0))) / math.sqrt(NB)
    row_pos = lax.broadcasted_iota(jnp.int32, (2, NB, NB), 1)
    col_pos = lax.broadcasted_iota(jnp.int32, (2, NB, NB), 2)
    values = jnp.where(col_pos > row_pos, offdiag, jnp.where(row_pos == col_pos, diagonal, 0.0))
    return values.astype(jnp.bfloat16)


def level_of(own_key, extent, shards, smallest, high):
    gain, own = 1.0, jax.random.fold_in(own_key, 6)
    for dim, parts in shards:
        draws = jnp.exp(jax.random.uniform(jax.random.fold_in(own, dim), (parts,), jnp.float32, smallest / len(shards), high / len(shards)))
        gain = gain * jnp.repeat(draws, extent[dim] // parts).reshape([-1 if axis == dim else 1 for axis in range(len(extent))])
    return gain


def gaussian(key, dims, scale, bound, cuts=(), dtype=jnp.bfloat16):
    gain = level_of(key, dims, cuts, -0.22, 0.18) if cuts else 1.0
    drawn = jax.random.normal(key, dims, jnp.float32) * scale * gain
    return jnp.minimum(jnp.maximum(drawn, -bound), bound).astype(dtype)


def setup_inputs(seed: int = 0) -> dict:
    key_of = jax.random.split(jax.random.key(seed), 4)
    return {
        "matrix": gaussian(key_of[0], (TR, N_ROW * NB, TC, N_COL * NB), 1.0, 6.0, ((1, 8), (3, 32))),
        "lower_inv": draw_lower_inv(jax.random.fold_in(key_of[3], 71), 0),
        "upper_inv": draw_upper_inv(jax.random.fold_in(key_of[3], 71), 0),
    }


def reference(matrix, lower_inv, upper_inv):
    whole = matrix.reshape(ROWS, COLS)
    lower_first = jnp.dot(whole[NB:, :NB], upper_inv[0], preferred_element_type=jnp.float32).astype(jnp.bfloat16)
    upper_first = jnp.dot(lower_inv[0], whole[:NB, NB:], preferred_element_type=jnp.float32).astype(jnp.bfloat16)
    column_next = (whole[2 * NB:, NB:2 * NB].astype(jnp.float32) - jnp.dot(lower_first[NB:], upper_first[:, :NB], preferred_element_type=jnp.float32)).astype(jnp.bfloat16)
    lower_second = jnp.dot(column_next, upper_inv[1], preferred_element_type=jnp.float32).astype(jnp.bfloat16)
    row_next = (whole[NB:2 * NB, 2 * NB:].astype(jnp.float32) - jnp.dot(lower_first[:NB], upper_first[:, NB:], preferred_element_type=jnp.float32)).astype(jnp.bfloat16)
    upper_second = jnp.dot(lower_inv[1], row_next, preferred_element_type=jnp.float32).astype(jnp.bfloat16)
    left = jnp.zeros((ROWS, 2 * NB), jnp.bfloat16).at[NB:, :NB].set(lower_first).at[2 * NB:, NB:].set(lower_second)
    right = jnp.zeros((2 * NB, COLS), jnp.bfloat16).at[:NB, NB:].set(upper_first).at[NB:, 2 * NB:].set(upper_second)

    def block_rows(pair):
        rows_a, rows_l = pair
        return (rows_a.astype(jnp.float32) - jnp.dot(rows_l, right, preferred_element_type=jnp.float32)).astype(jnp.bfloat16)

    blocks = lax.map(block_rows, (whole.reshape(ROWS // NB, NB, COLS), left.reshape(ROWS // NB, NB, 2 * NB)))
    factored = blocks.reshape(ROWS, COLS)
    factored = factored.at[NB:, :NB].set(lower_first)
    factored = factored.at[2 * NB:, NB:2 * NB].set(lower_second)
    factored = factored.at[:NB, NB:].set(upper_first)
    factored = factored.at[NB:2 * NB, 2 * NB:].set(upper_second)
    return factored.reshape(TR, N_ROW * NB, TC, N_COL * NB)
```

```python
import functools

import jax
import jax.numpy as jnp
from jax import lax
from jax.experimental import pallas as pl
from jax.experimental.pallas import tpu as pltpu
from jax.sharding import PartitionSpec as P

MESH = pl.DeviceIdType.MESH
F32, BF16 = jnp.float32, jnp.bfloat16
NB = 512
SIDE = 4
STEPS = ((1, 0), (0, 1), (-1, 0), (0, -1))
ENTERED = {
    (1, 0): 0, (2, 0): 0, (3, 0): 0, (0, 1): 2, (1, 1): 1, (2, 1): 0, (3, 1): 0, (0, 2): 2,
    (1, 2): 1, (2, 2): 0, (3, 2): 0, (0, 3): 2, (1, 3): 3, (2, 3): 3, (3, 3): 0,
}
CHUNK = 64
ZCHUNK = 32
LAG, ZLAG = 5, 5


def trees():
    def depth_of(chip):
        depth = 0
        while chip != (0, 0):
            dx, dy = STEPS[ENTERED[chip]]
            chip, depth = ((chip[0] - dx) % SIDE, (chip[1] - dy) % SIDE), depth + 1
        return depth

    depth = [[0] * SIDE**2 for _ in range(4)]
    owner = [[4] * SIDE**2 for _ in range(4)]
    for t in range(4):
        for chip, step in ENTERED.items():
            x, y = chip
            for _ in range(t):
                x, y = -y % SIDE, x
            d = (step + t) % 4
            depth[t][y * SIDE + x] = depth_of(chip)
            parent = (y - STEPS[d][1]) % SIDE * SIDE + (x - STEPS[d][0]) % SIDE
            owner[d][parent] = t
    return depth, owner


DEPTH, OWNER = trees()
DEEPEST = max(max(row) for row in DEPTH)


def pick(table, index):
    value = jnp.int32(table[-1])
    for i in range(len(table) - 2, -1, -1):
        value = jnp.where(index == i, jnp.int32(table[i]), value)
    return value


def dot(a, b):
    return jnp.dot(a, b, preferred_element_type=F32)


def kernel(
    tiles, n_row, n_col, m_ref, lower_ref, upper_ref, out_ref, o_ref, wide, panel, rows, extra,
    load_sem, store_sem, panel_recv, panel_send, pair_recv, pair_send, row_recv, row_send,
):
    z, col = lax.axis_index("row"), lax.axis_index("col")
    core, chip = col % 2, col // 2
    x, y = chip % SIDE, chip // SIDE
    root = chip == 0
    plain = tiles * NB // (4 * CHUNK)
    more = NB // (4 * CHUNK)
    count = plain + more
    zcount = NB // ZCHUNK
    lines = 8 * NB

    peers = []
    for dx, dy in STEPS:
        peers.append({"col": ((y + dy) % SIDE * SIDE + (x + dx) % SIDE) * 2 + core})
    pair = {"col": chip * 2 + 1 - core}
    ways = ({"row": (z + 1) % n_row}, {"row": (z + n_row - 1) % n_row})

    barrier = pltpu.get_barrier_semaphore()
    for device in (*peers, pair, *ways):
        pl.semaphore_signal(barrier, inc=1, device_id=device, device_id_type=MESH)

    def load(i):
        part = pl.ds(pl.multiple_of(i * lines, lines), lines)
        return pltpu.make_async_copy(m_ref.at[part], o_ref.at[part], load_sem.at[i])

    for i in range(tiles):
        load(i).start()

    def widen(i):
        load(i).wait()
        part = pl.ds(pl.multiple_of(i * lines, lines), lines)
        wide[part] = o_ref[part].astype(F32)

    def piece(first, length, j, c):
        return pl.ds(first * 8 + 2 * c + j, length, stride=8)

    def tile(first, length, j):
        return jnp.concatenate([wide[piece(first, length, j, c), :] for c in range(4)], axis=1)

    def own_column(i):
        first = pl.multiple_of(i * NB, NB)
        panel[core, pl.ds(first, NB)] = tile(first, NB, 0).astype(BF16)

    widen(0)
    for source in range(2):
        @pl.when(z == source)
        def _():
            for j in range(2):
                rows[source, j] = tile(0, NB, j).astype(BF16)

    @pl.when(root)
    def _():
        own_column(0)

    depth = [pick(DEPTH[t], chip) for t in range(4)]
    owner = [pick(OWNER[d], chip) for d in range(4)]
    sender = []
    for d in range(4):
        value = depth[3]
        for t in range(3):
            value = jnp.where(owner[d] == t, depth[t], value)
        sender.append(value)

    away = (z - (1 - core) + n_row) % n_row
    farthest = jnp.where(away == 0, 0, jnp.maximum(away, n_row - away))
    late = jnp.maximum(zcount // 2 + ZLAG * farthest, plain)
    last_late = max(zcount // 2 + ZLAG * (n_row - 1), plain)

    pl.semaphore_wait(barrier, len(peers) + 3)

    def panel_step(k, hops):
        step = k - LAG * hops
        step_late = step - late + plain
        return jnp.where(step_late >= plain, step_late, jnp.where(step < plain, step, count))

    def panel_copy(t, s, device, send):
        ref = panel.at[core, pl.ds(pl.multiple_of((s * 4 + t) * CHUNK, CHUNK), CHUNK)]
        return pltpu.make_async_remote_copy(
            ref, ref, send, panel_recv.at[t * count + s], device_id=device, device_id_type=MESH
        )

    def slot(k, carry):
        for order in range(2):
            which = (order + 1 - core) % 2
            for way in range(2):
                hops = (z - which + n_row) % n_row
                if way:
                    hops = (n_row - hops) % n_row
                s = k - order * zcount - ZLAG * hops

                @pl.when((s >= 0) & (s < zcount))
                def _():
                    j = s // (zcount // 2)
                    first = way * (NB // 2) + s % (zcount // 2) * ZCHUNK
                    ref = rows.at[which, j, pl.ds(pl.multiple_of(first, ZCHUNK), ZCHUNK)]
                    copy = pltpu.make_async_remote_copy(
                        ref, ref, row_send.at[order * 2 + way], row_recv.at[(order * 2 + way) * zcount + s],
                        device_id=ways[way], device_id_type=MESH,
                    )

                    @pl.when(hops > 0)
                    def _():
                        copy.wait_recv()

                    @pl.when(hops < n_row - 1)
                    def _():
                        copy.start()

        @pl.when(root & (k == late))
        def _():
            panel[core, pl.ds(tiles * NB, NB)] = rows[1 - core, 0]

        for t in range(4):
            s = panel_step(k, depth[t])

            @pl.when((s >= 0) & (s < count) & jnp.logical_not(root))
            def _():
                panel_copy(t, s, pair, pair_send.at[0]).wait_recv()

        for d in range(4):
            s = panel_step(k, sender[d])

            @pl.when((s >= 0) & (s < count) & (owner[d] < 4))
            def _():
                panel_copy(owner[d], s, peers[d], panel_send.at[d]).start()

        for t in range(4):
            s = panel_step(k, depth[t])

            @pl.when((s >= 0) & (s < count))
            def _():
                ref = panel.at[core, pl.ds(pl.multiple_of((s * 4 + t) * CHUNK, CHUNK), CHUNK)]
                pltpu.make_async_remote_copy(
                    ref, ref, pair_send.at[0], pair_recv.at[(s * 4 + t) * CHUNK // NB],
                    device_id=pair, device_id_type=MESH,
                ).start()

        after = k // more + 1

        @pl.when((k % more == 0) & (after < tiles))
        def _():
            widen(after)

            @pl.when(root)
            def _():
                own_column(after)

        return carry

    slots = max(last_late + more + LAG * DEEPEST, 2 * zcount + ZLAG * (n_row - 1))
    lax.fori_loop(0, slots, slot, 0)

    def drain(ref, sem):
        pltpu.make_async_copy(ref, ref, sem).wait()

    for i in range(tiles + 1):
        drain(panel.at[1 - core, pl.ds(i * NB, NB)], pair_recv.at[i])
    for d in range(4):
        @pl.when(owner[d] < 4)
        def _():
            drain(panel.at[core, pl.ds(0, count * CHUNK)], panel_send.at[d])
    drain(panel.at[core], pair_send.at[0])
    for order in range(2):
        for way in range(2):
            hops = (z - (order + 1 - core) % 2 + n_row) % n_row
            if way:
                hops = (n_row - hops) % n_row

            @pl.when(hops < n_row - 1)
            def _():
                drain(rows.at[order, 0], row_send.at[order * 2 + way])

    end = pl.ds(tiles * NB, NB)
    extra[0] = dot(panel[0, end], upper_ref[0]).astype(BF16)
    extra[1] = dot(lower_ref[0], panel[1, end]).astype(BF16)
    for j in range(2):
        rows[0, j] = dot(lower_ref[0], rows[0, j]).astype(BF16)
        following = rows[1, j].astype(F32) - dot(extra[0], rows[0, j])
        rows[1, j] = dot(lower_ref[1], following.astype(BF16)).astype(BF16)

    def finish(i, carry):
        first = pl.multiple_of(i * NB, NB)
        here = pl.ds(first, NB)
        panel[0, here] = dot(panel[0, here], upper_ref[0]).astype(BF16)
        following = panel[1, here].astype(F32) - dot(panel[0, here], extra[1])
        panel[1, here] = dot(following.astype(BF16), upper_ref[1]).astype(BF16)
        g = i * n_row + z
        for j in range(2):
            h = j * n_col + col

            def update(k):
                def block(b, carry):
                    at = pl.multiple_of(first + b * 128, 128)
                    product = dot(panel[k, pl.ds(at, 128)], rows[k, j])
                    for c in range(4):
                        where = piece(at, 128, j, c)
                        wide[where, :] = wide[where, :] - product[:, c * 128 : (c + 1) * 128]
                    return carry

                lax.fori_loop(0, NB // 128, block, 0)

            def replace(value):
                for c in range(4):
                    wide[piece(first, NB, j, c), :] = value[:, c * 128 : (c + 1) * 128].astype(F32)

            for k in range(2):
                pl.when((g > k) & (h > k))(functools.partial(update, k))
                pl.when((g > k) & (h == k))(lambda k=k: replace(panel[k, here]))
                pl.when((g == k) & (h > k))(lambda k=k: replace(rows[k, j]))
        part = pl.ds(pl.multiple_of(i * lines, lines), lines)
        o_ref[part] = wide[part].astype(BF16)
        pltpu.make_async_copy(o_ref.at[part], out_ref.at[part], store_sem.at[i]).start()
        return carry

    lax.fori_loop(0, tiles, finish, 0)
    for i in range(tiles):
        part = pl.ds(i * lines, lines)
        pltpu.make_async_copy(o_ref.at[part], out_ref.at[part], store_sem.at[i]).wait()


def on_device(n_row, n_col, matrix, lower_inv, upper_inv):
    tiles = matrix.shape[0]
    lines = tiles * NB * 8
    count = (tiles + 1) * NB // (4 * CHUNK)
    split = matrix.reshape(tiles, NB, 2, 4, 128).transpose(0, 1, 3, 2, 4).reshape(lines, 128)
    out = pl.pallas_call(
        functools.partial(kernel, tiles, n_row, n_col),
        out_shape=jax.ShapeDtypeStruct((lines, 128), BF16),
        in_specs=[
            pl.BlockSpec(memory_space=pl.ANY),
            pl.BlockSpec(memory_space=pltpu.VMEM),
            pl.BlockSpec(memory_space=pltpu.VMEM),
        ],
        out_specs=pl.BlockSpec(memory_space=pl.ANY),
        scratch_shapes=[
            pltpu.VMEM((lines, 128), BF16),
            pltpu.VMEM((lines, 128), F32),
            pltpu.VMEM((2, (tiles + 1) * NB, NB), BF16),
            pltpu.VMEM((2, 2, NB, NB), BF16),
            pltpu.VMEM((2, NB, NB), BF16),
            pltpu.SemaphoreType.DMA((tiles,)),
            pltpu.SemaphoreType.DMA((tiles,)),
            pltpu.SemaphoreType.DMA((4 * count,)),
            pltpu.SemaphoreType.DMA((4,)),
            pltpu.SemaphoreType.DMA((tiles + 1,)),
            pltpu.SemaphoreType.DMA((1,)),
            pltpu.SemaphoreType.DMA((4 * (NB // ZCHUNK),)),
            pltpu.SemaphoreType.DMA((4,)),
        ],
        compiler_params=pltpu.CompilerParams(
            collective_id=1, has_side_effects=True, vmem_limit_bytes=48 << 20
        ),
    )(split, lower_inv, upper_inv)
    return out.reshape(tiles, NB, 4, 2, 128).transpose(0, 1, 3, 2, 4).reshape(matrix.shape)


def solution(mesh):
    placed = (P(None, "row", None, "col"), P(), P())
    return jax.shard_map(
        functools.partial(on_device, mesh.shape["row"], mesh.shape["col"]),
        mesh=mesh,
        in_specs=placed,
        out_specs=P(None, "row", None, "col"),
        check_vma=False,
    )
```

```python
import functools

import jax
import jax.numpy as jnp
from jax import lax
from jax.experimental import pallas as pl
from jax.experimental.pallas import tpu as pltpu
from jax.sharding import PartitionSpec as P

MESH = pl.DeviceIdType.MESH
F32, BF16 = jnp.float32, jnp.bfloat16
NB = 512
SIDE = 4
STEPS = ((1, 0), (0, 1), (-1, 0), (0, -1))
ENTERED = {
    (1, 0): 0, (2, 0): 0, (3, 0): 0, (0, 1): 2, (1, 1): 1, (2, 1): 0, (3, 1): 0, (0, 2): 2,
    (1, 2): 1, (2, 2): 0, (3, 2): 0, (0, 3): 2, (1, 3): 3, (2, 3): 3, (3, 3): 0,
}
CHUNK = 64
ZCHUNK = 64
LAG, ZLAG = 4, 3


def trees():
    def depth_of(chip):
        depth = 0
        while chip != (0, 0):
            dx, dy = STEPS[ENTERED[chip]]
            chip, depth = ((chip[0] - dx) % SIDE, (chip[1] - dy) % SIDE), depth + 1
        return depth

    depth = [[0] * SIDE**2 for _ in range(4)]
    owner = [[4] * SIDE**2 for _ in range(4)]
    for t in range(4):
        for chip, step in ENTERED.items():
            x, y = chip
            for _ in range(t):
                x, y = -y % SIDE, x
            d = (step + t) % 4
            depth[t][y * SIDE + x] = depth_of(chip)
            parent = (y - STEPS[d][1]) % SIDE * SIDE + (x - STEPS[d][0]) % SIDE
            owner[d][parent] = t
    return depth, owner


DEPTH, OWNER = trees()
DEEPEST = max(max(row) for row in DEPTH)


def pick(table, index):
    value = jnp.int32(table[-1])
    for i in range(len(table) - 2, -1, -1):
        value = jnp.where(index == i, jnp.int32(table[i]), value)
    return value


def dot(a, b):
    return jnp.dot(a, b, preferred_element_type=F32)


def kernel(
    tiles, n_row, n_col, m_ref, lower_hbm, upper_hbm, out_ref, o_ref, wide, total, panel, low, rows, high, extra,
    lower_ref, upper_ref, load_sem, weight_sem, store_sem, panel_recv, panel_send, pair_recv, pair_send, row_recv, row_send,
):
    z, col = lax.axis_index("row"), lax.axis_index("col")
    core, chip = col % 2, col // 2
    x, y = chip % SIDE, chip // SIDE
    root = chip == 0
    plain = tiles * NB // (4 * CHUNK)
    more = NB // (4 * CHUNK)
    count = plain + more
    zcount = NB // ZCHUNK
    lines = 8 * NB

    peers = []
    for dx, dy in STEPS:
        peers.append({"col": ((y + dy) % SIDE * SIDE + (x + dx) % SIDE) * 2 + core})
    pair = {"col": chip * 2 + 1 - core}
    ways = ({"row": (z + 1) % n_row}, {"row": (z + n_row - 1) % n_row})

    barrier = pltpu.get_barrier_semaphore()
    for device in (*peers, pair, *ways):
        pl.semaphore_signal(barrier, inc=1, device_id=device, device_id_type=MESH)

    def load(i):
        part = pl.ds(pl.multiple_of(i * lines, lines), lines)
        return pltpu.make_async_copy(m_ref.at[part], o_ref.at[part], load_sem.at[i])

    weights = (
        pltpu.make_async_copy(lower_hbm, lower_ref, weight_sem.at[0]),
        pltpu.make_async_copy(upper_hbm, upper_ref, weight_sem.at[1]),
    )
    for i in range(tiles):
        load(i).start()
    for copy in weights:
        copy.start()

    def piece(first, length, j, c):
        return pl.ds(first * 8 + 2 * c + j, length, stride=8)

    def widen(i):
        load(i).wait()
        wide[...] = o_ref[pl.ds(pl.multiple_of(i * lines, lines), lines)].astype(F32)
        for j in range(2):
            for c in range(4):
                part = wide[piece(0, NB, j, c), :]
                total[j, pl.ds(pl.multiple_of(i * NB, NB), NB), c * 128 : (c + 1) * 128] = part

    def own_column(i):
        here = pl.ds(pl.multiple_of(i * NB, NB), NB)
        panel[core, here] = total[0, here].astype(BF16)

    widen(0)
    for source in range(2):
        @pl.when(z == source)
        def _():
            for j in range(2):
                rows[source, j] = total[j, pl.ds(0, NB)].astype(BF16)

    @pl.when(root)
    def _():
        own_column(0)

    depth = [pick(DEPTH[t], chip) for t in range(4)]
    owner = [pick(OWNER[d], chip) for d in range(4)]
    sender = []
    for d in range(4):
        value = depth[3]
        for t in range(3):
            value = jnp.where(owner[d] == t, depth[t], value)
        sender.append(value)

    away = (z - (1 - core) + n_row) % n_row
    farthest = jnp.where(away == 0, 0, jnp.maximum(away, n_row - away))
    late = jnp.maximum(zcount // 2 + ZLAG * farthest, plain)
    last_late = max(zcount // 2 + ZLAG * (n_row - 1), plain)

    pl.semaphore_wait(barrier, len(peers) + 3)

    def panel_step(k, hops):
        step = k - LAG * hops
        step_late = step - late + plain
        return jnp.where(step_late >= plain, step_late, jnp.where(step < plain, step, count))

    def panel_copy(t, s, device, send):
        ref = panel.at[core, pl.ds(pl.multiple_of((s * 4 + t) * CHUNK, CHUNK), CHUNK)]
        return pltpu.make_async_remote_copy(
            ref, ref, send, panel_recv.at[t * count + s], device_id=device, device_id_type=MESH
        )

    def slot(k, carry):
        for order in range(2):
            which = (order + 1 - core) % 2
            for way in range(2):
                hops = (z - which + n_row) % n_row
                if way:
                    hops = (n_row - hops) % n_row
                s = k - order * zcount - ZLAG * hops

                @pl.when((s >= 0) & (s < zcount))
                def _():
                    j = s // (zcount // 2)
                    first = way * (NB // 2) + s % (zcount // 2) * ZCHUNK
                    ref = rows.at[which, j, pl.ds(pl.multiple_of(first, ZCHUNK), ZCHUNK)]
                    copy = pltpu.make_async_remote_copy(
                        ref, ref, row_send.at[order * 2 + way], row_recv.at[(order * 2 + way) * zcount + s],
                        device_id=ways[way], device_id_type=MESH,
                    )

                    @pl.when(hops > 0)
                    def _():
                        copy.wait_recv()

                    @pl.when(hops < n_row - 1)
                    def _():
                        copy.start()

        @pl.when(root & (k == late))
        def _():
            panel[core, pl.ds(tiles * NB, NB)] = rows[1 - core, 0]

        for t in range(4):
            s = panel_step(k, depth[t])

            @pl.when((s >= 0) & (s < count) & jnp.logical_not(root))
            def _():
                panel_copy(t, s, pair, pair_send.at[0]).wait_recv()

        for d in range(4):
            s = panel_step(k, sender[d])

            @pl.when((s >= 0) & (s < count) & (owner[d] < 4))
            def _():
                panel_copy(owner[d], s, peers[d], panel_send.at[d]).start()

        for t in range(4):
            s = panel_step(k, depth[t])

            @pl.when((s >= 0) & (s < count))
            def _():
                ref = panel.at[core, pl.ds(pl.multiple_of((s * 4 + t) * CHUNK, CHUNK), CHUNK)]
                pltpu.make_async_remote_copy(
                    ref, ref, pair_send.at[0], pair_recv.at[(s * 4 + t) * CHUNK // NB],
                    device_id=pair, device_id_type=MESH,
                ).start()

        after = k // more + 1

        @pl.when((k % more == 0) & (after < tiles))
        def _():
            widen(after)

            @pl.when(root)
            def _():
                own_column(after)

        i = (k - first_low) // 2

        @pl.when((k >= first_low) & ((k - first_low) % 2 == 0) & (i < tiles))
        def _():
            here = pl.ds(pl.multiple_of(i * NB, NB), NB)

            @pl.when(core == 1)
            def _():
                drain(panel.at[0, here], pair_recv.at[i])

            low[here] = dot(panel[0, here], upper_ref[0]).astype(BF16)

        @pl.when((k >= rows_in) & (k < rows_in + 2))
        def _():
            high[k - rows_in] = dot(lower_ref[0], rows[0, k - rows_in]).astype(BF16)

        for b in range(3):
            unit = (k - rows_in - 2) * 3 + b
            i, j = unit // 4, unit // 2 % 2

            @pl.when((unit >= 0) & (unit < 4 * tiles) & (i * n_row + z > 0) & (j * n_col + col > 0))
            def _():
                half = pl.ds(pl.multiple_of(i * NB + unit % 2 * (NB // 2), NB // 2), NB // 2)
                total[j, half] = total[j, half] - dot(low[half], high[j])

        return carry

    def drain(ref, sem):
        pltpu.make_async_copy(ref, ref, sem).wait()

    for copy in weights:
        copy.wait()
    first_low = more - 1 + LAG * DEEPEST + 1
    rows_in = max(2 * zcount + ZLAG * (n_row - 1), first_low + 2 * tiles)
    slots = max(last_late + more + LAG * DEEPEST, rows_in + 2 + (4 * tiles + 2) // 3)
    lax.fori_loop(0, slots, slot, 0)

    for i in range(tiles):
        @pl.when(core == 0)
        def _():
            drain(panel.at[1, pl.ds(i * NB, NB)], pair_recv.at[i])
    drain(panel.at[1 - core, pl.ds(tiles * NB, NB)], pair_recv.at[tiles])
    for d in range(4):
        @pl.when(owner[d] < 4)
        def _():
            drain(panel.at[core, pl.ds(0, count * CHUNK)], panel_send.at[d])
    drain(panel.at[core], pair_send.at[0])
    for order in range(2):
        for way in range(2):
            hops = (z - (order + 1 - core) % 2 + n_row) % n_row
            if way:
                hops = (n_row - hops) % n_row

            @pl.when(hops < n_row - 1)
            def _():
                drain(rows.at[order, 0], row_send.at[order * 2 + way])

    end = pl.ds(tiles * NB, NB)
    extra[0] = dot(panel[0, end], upper_ref[0]).astype(BF16)
    extra[1] = dot(lower_ref[0], panel[1, end]).astype(BF16)
    for j in range(2):
        following = rows[1, j].astype(F32) - dot(extra[0], high[j])
        rows[1, j] = dot(lower_ref[1], following.astype(BF16)).astype(BF16)

    def finish(i, carry):
        first = pl.multiple_of(i * NB, NB)
        here = pl.ds(first, NB)
        following = panel[1, here].astype(F32) - dot(low[here], extra[1])
        panel[1, here] = dot(following.astype(BF16), upper_ref[1]).astype(BF16)
        g = i * n_row + z

        def spread(j, start, value):
            for c in range(4):
                wide[piece(start, value.shape[0], j, c), :] = value[:, c * 128 : (c + 1) * 128]

        for j in range(2):
            h = j * n_col + col
            both = (g > 1) & (h > 1)

            @pl.when(both)
            def _():
                for b in range(4):
                    at = pl.ds(pl.multiple_of(first + b * 128, 128), 128)
                    spread(j, b * 128, total[j, at] - dot(panel[1, at], rows[1, j]))

            @pl.when(jnp.logical_not(both))
            def _():
                @pl.when((g > 0) & (h == 0))
                def _():
                    total[j, here] = low[here].astype(F32)

                @pl.when((g > 1) & (h == 1))
                def _():
                    total[j, here] = panel[1, here].astype(F32)

                @pl.when((g == 0) & (h > 0))
                def _():
                    total[j, here] = high[j].astype(F32)

                @pl.when((g == 1) & (h > 1))
                def _():
                    total[j, here] = rows[1, j].astype(F32)

                spread(j, 0, total[j, here])

        part = pl.ds(pl.multiple_of(i * lines, lines), lines)
        o_ref[part] = wide[...].astype(BF16)
        pltpu.make_async_copy(o_ref.at[part], out_ref.at[part], store_sem.at[i]).start()
        return carry

    lax.fori_loop(0, tiles, finish, 0)
    for i in range(tiles):
        part = pl.ds(i * lines, lines)
        pltpu.make_async_copy(o_ref.at[part], out_ref.at[part], store_sem.at[i]).wait()


def hand_on(x_ref, o_ref):
    o_ref[...] = x_ref[...]


def on_device(n_row, n_col, matrix, lower_inv, upper_inv):
    tiles = matrix.shape[0]
    lines = tiles * NB * 8
    count = (tiles + 1) * NB // (4 * CHUNK)
    split = matrix.reshape(tiles, NB, 2, 4, 128).transpose(0, 1, 3, 2, 4).reshape(lines, 128)
    out = pl.pallas_call(
        functools.partial(kernel, tiles, n_row, n_col),
        out_shape=jax.ShapeDtypeStruct((lines, 128), BF16),
        in_specs=[
            pl.BlockSpec(memory_space=pltpu.HBM),
            pl.BlockSpec(memory_space=pltpu.HBM),
            pl.BlockSpec(memory_space=pltpu.HBM),
        ],
        out_specs=pl.BlockSpec(memory_space=pl.ANY),
        scratch_shapes=[
            pltpu.VMEM((lines, 128), BF16),
            pltpu.VMEM((8 * NB, 128), F32),
            pltpu.VMEM((2, tiles * NB, NB), F32),
            pltpu.VMEM((2, (tiles + 1) * NB, NB), BF16),
            pltpu.VMEM((tiles * NB, NB), BF16),
            pltpu.VMEM((2, 2, NB, NB), BF16),
            pltpu.VMEM((2, NB, NB), BF16),
            pltpu.VMEM((2, NB, NB), BF16),
            pltpu.VMEM((2, NB, NB), BF16),
            pltpu.VMEM((2, NB, NB), BF16),
            pltpu.SemaphoreType.DMA((tiles,)),
            pltpu.SemaphoreType.DMA((2,)),
            pltpu.SemaphoreType.DMA((tiles,)),
            pltpu.SemaphoreType.DMA((4 * count,)),
            pltpu.SemaphoreType.DMA((4,)),
            pltpu.SemaphoreType.DMA((tiles + 1,)),
            pltpu.SemaphoreType.DMA((1,)),
            pltpu.SemaphoreType.DMA((4 * (NB // ZCHUNK),)),
            pltpu.SemaphoreType.DMA((4,)),
        ],
        compiler_params=pltpu.CompilerParams(
            collective_id=1, has_side_effects=True, vmem_limit_bytes=48 << 20
        ),
    )(split, lower_inv, upper_inv)
    block = pl.BlockSpec((NB * 16, 128), lambda i: (i, 0))
    out = pl.pallas_call(
        hand_on,
        out_shape=jax.ShapeDtypeStruct((lines, 128), BF16),
        grid=(lines // (NB * 16),),
        in_specs=[block],
        out_specs=block,
        compiler_params=pltpu.CompilerParams(vmem_limit_bytes=32 << 20),
    )(out)
    return out.reshape(tiles, NB, 4, 2, 128).transpose(0, 1, 3, 2, 4).reshape(matrix.shape)


def solution(mesh):
    placed = (P(None, "row", None, "col"), P(), P())
    return jax.shard_map(
        functools.partial(on_device, mesh.shape["row"], mesh.shape["col"]),
        mesh=mesh,
        in_specs=placed,
        out_specs=P(None, "row", None, "col"),
        check_vma=False,
    )
```

```python
import functools

import jax
import jax.numpy as jnp
from jax import lax
from jax.experimental import pallas as pl
from jax.experimental.pallas import tpu as pltpu
from jax.sharding import PartitionSpec as P

MESH = pl.DeviceIdType.MESH
F32, BF16 = jnp.float32, jnp.bfloat16
NB = 512
SIDE = 4
STEPS = ((1, 0), (0, 1), (-1, 0), (0, -1))
ENTERED = {
    (1, 0): 0, (2, 0): 0, (3, 0): 0, (0, 1): 2, (1, 1): 1, (2, 1): 0, (3, 1): 0, (0, 2): 2,
    (1, 2): 1, (2, 2): 0, (3, 2): 0, (0, 3): 2, (1, 3): 3, (2, 3): 3, (3, 3): 0,
}
CHUNK = 64
ZCHUNK = 64
LAG, ZLAG = 4, 3


def trees():
    def depth_of(chip):
        depth = 0
        while chip != (0, 0):
            dx, dy = STEPS[ENTERED[chip]]
            chip, depth = ((chip[0] - dx) % SIDE, (chip[1] - dy) % SIDE), depth + 1
        return depth

    depth = [[0] * SIDE**2 for _ in range(4)]
    owner = [[4] * SIDE**2 for _ in range(4)]
    for t in range(4):
        for chip, step in ENTERED.items():
            x, y = chip
            for _ in range(t):
                x, y = -y % SIDE, x
            d = (step + t) % 4
            depth[t][y * SIDE + x] = depth_of(chip)
            parent = (y - STEPS[d][1]) % SIDE * SIDE + (x - STEPS[d][0]) % SIDE
            owner[d][parent] = t
    return depth, owner


DEPTH, OWNER = trees()
DEEPEST = max(max(row) for row in DEPTH)


def pick(table, index):
    value = jnp.int32(table[-1])
    for i in range(len(table) - 2, -1, -1):
        value = jnp.where(index == i, jnp.int32(table[i]), value)
    return value


def dot(a, b):
    return jnp.dot(a, b, preferred_element_type=F32)


def kernel(
    tiles, n_row, n_col, m_ref, lower_hbm, upper_hbm, out_ref, o_ref, wide, total, panel, low, rows, high, extra,
    lower_ref, upper_ref, load_sem, weight_sem, store_sem, panel_recv, panel_send, pair_recv, pair_send, row_recv, row_send,
):
    z, col = lax.axis_index("row"), lax.axis_index("col")
    core, chip = col % 2, col // 2
    x, y = chip % SIDE, chip // SIDE
    root = chip == 0
    plain = tiles * NB // (4 * CHUNK)
    more = NB // (4 * CHUNK)
    count = plain + more
    zcount = NB // ZCHUNK
    lines = 8 * NB

    peers = []
    for dx, dy in STEPS:
        peers.append({"col": ((y + dy) % SIDE * SIDE + (x + dx) % SIDE) * 2 + core})
    pair = {"col": chip * 2 + 1 - core}
    ways = ({"row": (z + 1) % n_row}, {"row": (z + n_row - 1) % n_row})

    barrier = pltpu.get_barrier_semaphore()
    for device in (*peers, pair, *ways):
        pl.semaphore_signal(barrier, inc=1, device_id=device, device_id_type=MESH)

    def load(i):
        part = pl.ds(pl.multiple_of(i * lines, lines), lines)
        return pltpu.make_async_copy(m_ref.at[part], o_ref.at[part], load_sem.at[i])

    weights = (
        pltpu.make_async_copy(lower_hbm, lower_ref, weight_sem.at[0]),
        pltpu.make_async_copy(upper_hbm, upper_ref, weight_sem.at[1]),
    )
    for i in range(tiles):
        load(i).start()
    for copy in weights:
        copy.start()

    def piece(first, length, j, c):
        return pl.ds(first * 8 + 2 * c + j, length, stride=8)

    def widen(i):
        load(i).wait()
        wide[...] = o_ref[pl.ds(pl.multiple_of(i * lines, lines), lines)].astype(F32)
        for j in range(2):
            for c in range(4):
                part = wide[piece(0, NB, j, c), :]
                total[j, pl.ds(pl.multiple_of(i * NB, NB), NB), c * 128 : (c + 1) * 128] = part

    def own_column(i):
        here = pl.ds(pl.multiple_of(i * NB, NB), NB)
        panel[core, here] = total[0, here].astype(BF16)

    widen(0)
    for source in range(2):
        @pl.when(z == source)
        def _():
            for j in range(2):
                rows[source, j] = total[j, pl.ds(0, NB)].astype(BF16)

    @pl.when(root)
    def _():
        own_column(0)

    depth = [pick(DEPTH[t], chip) for t in range(4)]
    owner = [pick(OWNER[d], chip) for d in range(4)]
    sender = []
    for d in range(4):
        value = depth[3]
        for t in range(3):
            value = jnp.where(owner[d] == t, depth[t], value)
        sender.append(value)

    away = (z - (1 - core) + n_row) % n_row
    farthest = jnp.where(away == 0, 0, jnp.maximum(away, n_row - away))
    late = jnp.maximum(zcount // 2 + ZLAG * farthest, plain)
    last_late = max(zcount // 2 + ZLAG * (n_row - 1), plain)

    pl.semaphore_wait(barrier, len(peers) + 3)

    def panel_step(k, hops):
        step = k - LAG * hops
        step_late = step - late + plain
        return jnp.where(step_late >= plain, step_late, jnp.where(step < plain, step, count))

    def panel_copy(t, s, device, send):
        ref = panel.at[core, pl.ds(pl.multiple_of((s * 4 + t) * CHUNK, CHUNK), CHUNK)]
        return pltpu.make_async_remote_copy(
            ref, ref, send, panel_recv.at[t * count + s], device_id=device, device_id_type=MESH
        )

    def slot(k, carry):
        for order in range(2):
            which = (order + 1 - core) % 2
            for way in range(2):
                hops = (z - which + n_row) % n_row
                if way:
                    hops = (n_row - hops) % n_row
                s = k - order * zcount - ZLAG * hops

                @pl.when((s >= 0) & (s < zcount))
                def _():
                    j = s // (zcount // 2)
                    first = way * (NB // 2) + s % (zcount // 2) * ZCHUNK
                    ref = rows.at[which, j, pl.ds(pl.multiple_of(first, ZCHUNK), ZCHUNK)]
                    copy = pltpu.make_async_remote_copy(
                        ref, ref, row_send.at[order * 2 + way], row_recv.at[(order * 2 + way) * zcount + s],
                        device_id=ways[way], device_id_type=MESH,
                    )

                    @pl.when(hops > 0)
                    def _():
                        copy.wait_recv()

                    @pl.when(hops < n_row - 1)
                    def _():
                        copy.start()

        @pl.when(root & (k == late))
        def _():
            panel[core, pl.ds(tiles * NB, NB)] = rows[1 - core, 0]

        for t in range(4):
            s = panel_step(k, depth[t])

            @pl.when((s >= 0) & (s < count) & jnp.logical_not(root))
            def _():
                panel_copy(t, s, pair, pair_send.at[0]).wait_recv()

        for d in range(4):
            s = panel_step(k, sender[d])

            @pl.when((s >= 0) & (s < count) & (owner[d] < 4))
            def _():
                panel_copy(owner[d], s, peers[d], panel_send.at[d]).start()

        for t in range(4):
            s = panel_step(k, depth[t])

            @pl.when((s >= 0) & (s < count))
            def _():
                ref = panel.at[core, pl.ds(pl.multiple_of((s * 4 + t) * CHUNK, CHUNK), CHUNK)]
                pltpu.make_async_remote_copy(
                    ref, ref, pair_send.at[0], pair_recv.at[(s * 4 + t) * CHUNK // NB],
                    device_id=pair, device_id_type=MESH,
                ).start()

        after = k // more + 1

        @pl.when((k % more == 0) & (after < tiles))
        def _():
            widen(after)

            @pl.when(root)
            def _():
                own_column(after)

        i = (k - first_low) // 2

        @pl.when((k >= first_low) & ((k - first_low) % 2 == 0) & (i < tiles))
        def _():
            here = pl.ds(pl.multiple_of(i * NB, NB), NB)

            @pl.when(core == 1)
            def _():
                drain(panel.at[0, here], pair_recv.at[i])

            low[here] = dot(panel[0, here], upper_ref[0]).astype(BF16)

        @pl.when((k >= rows_in) & (k < rows_in + 2))
        def _():
            high[k - rows_in] = dot(lower_ref[0], rows[0, k - rows_in]).astype(BF16)

        for b in range(3):
            unit = (k - rows_in - 2) * 3 + b
            i, j = unit // 4, unit // 2 % 2

            @pl.when((unit >= 0) & (unit < 4 * tiles) & (i * n_row + z > 0) & (j * n_col + col > 0))
            def _():
                half = pl.ds(pl.multiple_of(i * NB + unit % 2 * (NB // 2), NB // 2), NB // 2)
                total[j, half] = total[j, half] - dot(low[half], high[j])

        return carry

    def drain(ref, sem):
        pltpu.make_async_copy(ref, ref, sem).wait()

    for copy in weights:
        copy.wait()
    first_low = more - 1 + LAG * DEEPEST + 1
    rows_in = max(2 * zcount + ZLAG * (n_row - 1), first_low + 2 * tiles)
    slots = max(last_late + more + LAG * DEEPEST, rows_in + 2 + (4 * tiles + 2) // 3)
    lax.fori_loop(0, slots, slot, 0)

    for i in range(tiles):
        @pl.when(core == 0)
        def _():
            drain(panel.at[1, pl.ds(i * NB, NB)], pair_recv.at[i])
    drain(panel.at[1 - core, pl.ds(tiles * NB, NB)], pair_recv.at[tiles])
    for d in range(4):
        @pl.when(owner[d] < 4)
        def _():
            drain(panel.at[core, pl.ds(0, count * CHUNK)], panel_send.at[d])
    drain(panel.at[core], pair_send.at[0])
    for order in range(2):
        for way in range(2):
            hops = (z - (order + 1 - core) % 2 + n_row) % n_row
            if way:
                hops = (n_row - hops) % n_row

            @pl.when(hops < n_row - 1)
            def _():
                drain(rows.at[order, 0], row_send.at[order * 2 + way])

    end = pl.ds(tiles * NB, NB)
    extra[0] = dot(panel[0, end], upper_ref[0]).astype(BF16)
    extra[1] = dot(lower_ref[0], panel[1, end]).astype(BF16)
    for j in range(2):
        following = rows[1, j].astype(F32) - dot(extra[0], high[j])
        rows[1, j] = dot(lower_ref[1], following.astype(BF16)).astype(BF16)

    def finish(i, carry):
        first = pl.multiple_of(i * NB, NB)
        here = pl.ds(first, NB)
        g = i * n_row + z
        inner = (g > 1) & (col > 1)

        def spread(j, start, value):
            for c in range(4):
                wide[piece(start, value.shape[0], j, c), :] = value[:, c * 128 : (c + 1) * 128]

        def solve(at):
            following = panel[1, at].astype(F32) - dot(low[at], extra[1])
            return dot(following.astype(BF16), upper_ref[1]).astype(BF16)

        @pl.when(inner)
        def _():
            for b in range(2):
                at = pl.ds(pl.multiple_of(first + b * 256, 256), 256)
                lower = solve(at)
                for j in range(2):
                    spread(j, b * 256, total[j, at] - dot(lower, rows[1, j]))

        @pl.when(jnp.logical_not(inner))
        def _():
            panel[1, here] = solve(here)

        for j in range(2):
            h = j * n_col + col
            both = (g > 1) & (h > 1)

            @pl.when(both & jnp.logical_not(inner))
            def _():
                for b in range(2):
                    at = pl.ds(pl.multiple_of(first + b * 256, 256), 256)
                    spread(j, b * 256, total[j, at] - dot(panel[1, at], rows[1, j]))

            @pl.when(jnp.logical_not(both))
            def _():
                @pl.when((g > 0) & (h == 0))
                def _():
                    total[j, here] = low[here].astype(F32)

                @pl.when((g > 1) & (h == 1))
                def _():
                    total[j, here] = panel[1, here].astype(F32)

                @pl.when((g == 0) & (h > 0))
                def _():
                    total[j, here] = high[j].astype(F32)

                @pl.when((g == 1) & (h > 1))
                def _():
                    total[j, here] = rows[1, j].astype(F32)

                spread(j, 0, total[j, here])

        part = pl.ds(pl.multiple_of(i * lines, lines), lines)
        o_ref[part] = wide[...].astype(BF16)
        pltpu.make_async_copy(o_ref.at[part], out_ref.at[part], store_sem.at[i]).start()
        return carry

    lax.fori_loop(0, tiles, finish, 0)
    for i in range(tiles):
        part = pl.ds(i * lines, lines)
        pltpu.make_async_copy(o_ref.at[part], out_ref.at[part], store_sem.at[i]).wait()


def hand_on(x_ref, o_ref):
    o_ref[...] = x_ref[...]


def on_device(n_row, n_col, matrix, lower_inv, upper_inv):
    tiles = matrix.shape[0]
    lines = tiles * NB * 8
    count = (tiles + 1) * NB // (4 * CHUNK)
    split = matrix.reshape(tiles, NB, 2, 4, 128).transpose(0, 1, 3, 2, 4).reshape(lines, 128)
    out = pl.pallas_call(
        functools.partial(kernel, tiles, n_row, n_col),
        out_shape=jax.ShapeDtypeStruct((lines, 128), BF16),
        in_specs=[
            pl.BlockSpec(memory_space=pltpu.HBM),
            pl.BlockSpec(memory_space=pltpu.HBM),
            pl.BlockSpec(memory_space=pltpu.HBM),
        ],
        out_specs=pl.BlockSpec(memory_space=pl.ANY),
        scratch_shapes=[
            pltpu.VMEM((lines, 128), BF16),
            pltpu.VMEM((8 * NB, 128), F32),
            pltpu.VMEM((2, tiles * NB, NB), F32),
            pltpu.VMEM((2, (tiles + 1) * NB, NB), BF16),
            pltpu.VMEM((tiles * NB, NB), BF16),
            pltpu.VMEM((2, 2, NB, NB), BF16),
            pltpu.VMEM((2, NB, NB), BF16),
            pltpu.VMEM((2, NB, NB), BF16),
            pltpu.VMEM((2, NB, NB), BF16),
            pltpu.VMEM((2, NB, NB), BF16),
            pltpu.SemaphoreType.DMA((tiles,)),
            pltpu.SemaphoreType.DMA((2,)),
            pltpu.SemaphoreType.DMA((tiles,)),
            pltpu.SemaphoreType.DMA((4 * count,)),
            pltpu.SemaphoreType.DMA((4,)),
            pltpu.SemaphoreType.DMA((tiles + 1,)),
            pltpu.SemaphoreType.DMA((1,)),
            pltpu.SemaphoreType.DMA((4 * (NB // ZCHUNK),)),
            pltpu.SemaphoreType.DMA((4,)),
        ],
        compiler_params=pltpu.CompilerParams(
            collective_id=1, has_side_effects=True, vmem_limit_bytes=60 << 20
        ),
    )(split, lower_inv, upper_inv)
    block = pl.BlockSpec((NB * 16, 128), lambda i: (i, 0))
    out = pl.pallas_call(
        hand_on,
        out_shape=jax.ShapeDtypeStruct((lines, 128), BF16),
        grid=(lines // (NB * 16),),
        in_specs=[block],
        out_specs=block,
        compiler_params=pltpu.CompilerParams(vmem_limit_bytes=32 << 20),
    )(out)
    return out.reshape(tiles, NB, 4, 2, 128).transpose(0, 1, 3, 2, 4).reshape(matrix.shape)


def solution(mesh):
    placed = (P(None, "row", None, "col"), P(), P())
    return jax.shard_map(
        functools.partial(on_device, mesh.shape["row"], mesh.shape["col"]),
        mesh=mesh,
        in_specs=placed,
        out_specs=P(None, "row", None, "col"),
        check_vma=False,
    )
```
